128 devices in a mesh: dp: 8 (over y, core), row: 8 (over x_hi, z), col: 2 (over x_lo).
Axes of the slice: x: 4 (x_hi: 2, x_lo: 2; x = x_hi * 2 + x_lo), y: 4, z: 4, core: 2. Of those that a mesh axis runs over, the one named last changes fastest.
Arguments:
- x_in: bfloat16 [1088, 16384], P(('row', 'col'), 'dp'), may hold values from -14 to 14
- segment_ids: int32 [16384], replicated, may hold values from 0 to 8, as said below
- attention_norm_gain: float32 [1, 1088], P(None, ('row', 'col')), may hold values from 0.5 to 1.5
- norm1_bias: float32 [1, 1088], P(None, ('row', 'col')), may hold values from -2.5 to 2.5
- w_qkv: bfloat16 [1, 1088, 3264], P(None, 'row', 'col'), may hold values from -0.1875 to 0.1875
- w_attn_out: bfloat16 [1, 1088, 1088], P(None, 'row', 'col'), may hold values from -3 to 3
- feedforward_norm_gain: float32 [1, 1088], P(None, ('row', 'col')), may hold values from 0.5 to 1.5
- norm2_bias: float32 [1, 1088], P(None, ('row', 'col')), may hold values from -2.5 to 2.5
- w_up: bfloat16 [1, 1088, 4352], P(None, 'row', 'col'), may hold values from -0.1875 to 0.1875
- w_down: bfloat16 [1, 1088, 4352], P(None, 'row', 'col'), may hold values from -0.09375 to 0.09375
- cotangent: float32 [1088, 16384], P(('row', 'col'), 'dp'), may hold values from -6 to 6
Outputs:
- block_out: float32 [1088, 16384], P(('row', 'col'), 'dp')
- grad_input: float32 [1088, 16384], P(('row', 'col'), 'dp')
- grad_norm1_gain: float32 [1, 1088], P(None, ('row', 'col'))
- grad_norm1_bias: float32 [1, 1088], P(None, ('row', 'col'))
- grad_qkv: float32 [1, 1088, 3264], P(None, 'row', 'col')
- grad_attn_out: float32 [1, 1088, 1088], P(None, 'row', 'col')
- grad_norm2_gain: float32 [1, 1088], P(None, ('row', 'col'))
- grad_norm2_bias: float32 [1, 1088], P(None, ('row', 'col'))
- grad_up: float32 [1, 1088, 4352], P(None, 'row', 'col')
- grad_down: float32 [1, 1088, 4352], P(None, 'row', 'col')
The draws below stay inside these ranges and needn't reach their ends.
Inputs may be any that keep to these rules, and one draw needn't show every extreme that they name: `segment_ids`: ids never fall along the stream. The first document holds between 512 and 1536 tokens, every later one exactly 2048 tokens but the last, which the end of the stream cuts.
All inputs are finite; a program needn't handle non-finite values.
Results may differ from the reference program's by a relative error of at most 0.0087.
Values may be sent and summed in bfloat16 or wider, within the bound.
No kernel may reach another device: no remote copies, remote signals or barrier semaphores. Data moves between devices by JAX's collectives and lax.ppermute only.
A program may use at most 256 MiB of HBM per device.

```python
import math
import jax
import jax.numpy as jnp
from jax import lax

D = 1088
HEADS = 17
HEAD_DIM = 64
FF = 4352
LAYERS = 1
SEQ = 2048
TOKENS = 16384


def draw_x_in(key, part):
    key = jax.random.fold_in(key, 11)
    profile = jnp.exp(math.log(3.0) * jnp.arange(D, dtype=jnp.float32) / D)
    values = jnp.clip(jax.random.normal(key, (TOKENS, D), jnp.float32), -6.0, 6.0)
    result = values * profile * 0.6
    return result.T.astype(jnp.bfloat16)


def draw_segment_ids(key, part):
    key = jax.random.fold_in(key, 23)
    offset = jax.random.randint(key, (), SEQ // 4, 3 * SEQ // 4 + 1, jnp.int32)
    return ((jnp.arange(TOKENS, dtype=jnp.int32) + SEQ - offset) // SEQ).astype(jnp.int32)


def block_scale(own_key, dims, shards, low, largest):
    factor_of, own = 1.0, jax.random.fold_in(own_key, 6)
    for axis_at, shards_of in shards:
        heights = jnp.exp(jax.random.uniform(jax.random.fold_in(own, axis_at), (shards_of,), jnp.float32, low / len(shards), largest / len(shards)))
        factor_of = factor_of * jnp.repeat(heights, dims[axis_at] // shards_of).reshape([-1 if axis == axis_at else 1 for axis in range(len(dims))])
    return factor_of


def scatter_about(rng, shape, scale, limit, cuts=(), kind=jnp.bfloat16):
    values = jax.random.normal(rng, shape, jnp.float32) * scale
    if len(cuts) > 0:
        values = block_scale(rng, shape, cuts, -0.22, 0.18) * values
    return jnp.clip(values, min=-limit, max=limit).astype(kind)


def setup_inputs(seed: int = 0) -> dict:
    splits = jax.random.split(jax.random.key(seed), 12)
    x_in = draw_x_in(jax.random.fold_in(splits[11], 71), 0)
    segment_ids = draw_segment_ids(jax.random.fold_in(splits[11], 71), 0)
    attention_norm_gain = jnp.clip(0.5 + 1.0 * jax.random.uniform(splits[2], (LAYERS, D), jnp.float32) ** block_scale(splits[2], (LAYERS, D), ((1, 16),), -0.2, 0.2), 0.5, 1.5)
    norm1_bias = scatter_about(splits[3], (LAYERS, D), 0.3, 2.5, ((1, 16),), jnp.float32)
    w_qkv = scatter_about(splits[4], (LAYERS, D, 3 * D), D ** -0.5, 0.1875, ((1, 8), (2, 2)))
    w_attn_out = scatter_about(splits[5], (LAYERS, D, D), (max(D // 256, 1)) ** -0.5, 3.0, ((1, 8), (2, 2)))
    feedforward_norm_gain = jnp.clip(0.5 + 1.0 * jax.random.uniform(splits[6], (LAYERS, D), jnp.float32) ** block_scale(splits[6], (LAYERS, D), ((1, 16),), -0.2, 0.2), 0.5, 1.5)
    norm2_bias = scatter_about(splits[7], (LAYERS, D), 0.3, 2.5, ((1, 16),), jnp.float32)
    w_up = scatter_about(splits[8], (LAYERS, D, FF), D ** -0.5, 0.1875, ((1, 8), (2, 2)))
    w_down = scatter_about(splits[9], (LAYERS, D, FF), FF ** -0.5, 0.09375, ((1, 8), (2, 2)))
    cotangent = scatter_about(splits[10], (D, TOKENS), 1.0, 6.0, ((0, 16), (1, 8)), jnp.float32)
    return dict(x_in=x_in, segment_ids=segment_ids, attention_norm_gain=attention_norm_gain, norm1_bias=norm1_bias, w_qkv=w_qkv, w_attn_out=w_attn_out, feedforward_norm_gain=feedforward_norm_gain, norm2_bias=norm2_bias, w_up=w_up, w_down=w_down, cotangent=cotangent)


@jax.custom_vjp
def low(v):
    return lax.optimization_barrier(v.astype(jnp.bfloat16)).astype(jnp.float32)

@jax.custom_vjp
def low_back(v):
    return v

def low_keep(v):
    return (low(v), None)

def low_pass(kept, grad):
    return (grad,)

def back_keep(v):
    return (v, None)

def back_low(kept, grad):
    return (low(grad),)
low.defvjp(low_keep, low_pass)
low_back.defvjp(back_keep, back_low)

def product(left, right):
    return jnp.dot(left, right, preferred_element_type=jnp.float32, precision=lax.Precision.HIGHEST)

def gelu_tanh(value):
    return jax.nn.gelu(value, approximate=True)

def layer_norm(stream, gain, bias):
    average = lax.optimization_barrier(jnp.mean(stream, -1, keepdims=True))
    centred = stream - average
    spread = lax.optimization_barrier(jnp.mean(centred * centred, -1, keepdims=True))
    return centred * lax.rsqrt(spread + 1e-05) * gain + bias

def attention(mixed, padded_ids):
    queries = mixed[:, :D]
    context = jnp.concatenate([jnp.zeros((SEQ, 2 * D), jnp.float32), mixed[:, D:]], 0)
    query_pos = jnp.arange(SEQ, dtype=jnp.int32)
    key_pos = jnp.arange(2 * SEQ, dtype=jnp.int32)
    scaling = 1.0 / math.sqrt(HEAD_DIM)

    def one_block(block_no):
        start = (block_no * SEQ).astype(jnp.int32)
        query_rows = lax.dynamic_slice_in_dim(queries, start, SEQ, 0).reshape(SEQ, HEADS, HEAD_DIM)
        context_rows = lax.dynamic_slice_in_dim(context, start, 2 * SEQ, 0)
        key_rows = context_rows[:, :D].reshape(2 * SEQ, HEADS, HEAD_DIM)
        value_rows = context_rows[:, D:].reshape(2 * SEQ, HEADS, HEAD_DIM)
        query_ids = lax.dynamic_slice_in_dim(padded_ids, start + SEQ, SEQ, 0)
        key_ids = lax.dynamic_slice_in_dim(padded_ids, start, 2 * SEQ, 0)
        allowed = (query_ids[:, None] == key_ids[None, :]) & (key_pos[None, :] <= query_pos[:, None] + SEQ)
        scores = jnp.einsum('qhd,khd->hqk', query_rows, key_rows, precision=lax.Precision.HIGHEST) * scaling
        scores = jnp.where(allowed[None], low_back(scores), -1e+30)
        probs = low(jax.nn.softmax(scores, -1))
        attended = jnp.einsum('hqk,khd->qhd', probs, value_rows, precision=lax.Precision.HIGHEST)
        return attended.reshape(SEQ, D)
    blocks = lax.map(jax.checkpoint(one_block), jnp.arange(TOKENS // SEQ, dtype=jnp.int32))
    return blocks.reshape(TOKENS, D)

def block_forward(stream, gain_one, bias_one, w_mix, w_out, gain_two, bias_two, w_in, w_back, padded_ids):
    normalized_input = low(layer_norm(stream, gain_one, bias_one))
    mixed = low_back(low(product(normalized_input, w_mix)))
    attended = low_back(low(attention(mixed, padded_ids)))
    middle = stream + low_back(product(attended, w_out.T))
    normalized_middle = low(layer_norm(middle, gain_two, bias_two))
    before = low_back(product(normalized_middle, w_in))
    hidden = low(gelu_tanh(before))
    return middle + low_back(product(hidden, w_back.T))

def reference(x_in, segment_ids, attention_norm_gain, norm1_bias, w_qkv, w_attn_out, feedforward_norm_gain, norm2_bias, w_up, w_down, cotangent):
    padded_ids = jnp.concatenate([jnp.full((SEQ,), -1, jnp.int32), segment_ids.astype(jnp.int32)])
    weights = tuple((member.astype(jnp.float32) for member in (attention_norm_gain, norm1_bias, w_qkv, w_attn_out, feedforward_norm_gain, norm2_bias, w_up, w_down)))

    def forward(stream_t, params):
        stream = stream_t.T
        for layer_position in range(LAYERS):
            stream = block_forward(stream, *[member[layer_position] for member in params], padded_ids)
        return stream.T
    block_out, pullback = jax.vjp(forward, x_in.astype(jnp.float32), weights)
    grad_input, grads = pullback(cotangent.astype(jnp.float32))
    return (block_out, grad_input, grads[0], grads[1], grads[2], grads[3], grads[4], grads[5], grads[6], grads[7])
```

```python
import functools
import itertools
import math

import jax
import jax.numpy as jnp
from jax import lax
from jax.experimental import pallas as pl
from jax.experimental.pallas import tpu as pltpu
from jax.sharding import Mesh, PartitionSpec as P

HEADS = 17
HEAD_DIM = 64
PAIR_HEADS = HEADS - 1
epsilon = 1e-05
LOG2E = math.log2(math.e)
NEG = -1e30
AXES = ("y", "k", "xh", "z", "xl")
SIZES = (4, 2, 2, 4, 2)
PLANE = ("xh", "z", "xl")
ROW = ("xh", "z")
SLOTS = 16
F32 = jnp.float32
BF16 = jnp.bfloat16


def hop(value, dest):
    spots = list(itertools.product(*[range(s) for s in SIZES]))
    at = {c: i for i, c in enumerate(spots)}
    pairs = [(at[c], at[dest(*c)]) for c in spots if dest(*c) is not None]
    return lax.ppermute(value, AXES, pairs)


def other_core(value):
    return hop(value, lambda y, k, xh, z, xl: (y, 1 - k, xh, z, xl))


def to_group(value, by):
    def dest(y, k, xh, z, xl):
        g = (2 * y + k + by) % 8
        return (g // 2, g % 2, xh, z, xl)

    return hop(value, dest)


def match_half(value):
    def dest(y, k, xh, z, xl):
        return (y, k, xh, z, xl) if k == xl else (y, 1 - k, xh, z, 1 - xl)

    return hop(value, dest)


def beside(value):
    return hop(value, lambda y, k, xh, z, xl: (y, k, xh, z, 1 - xl))


def along_z(value, by):
    return hop(value, lambda y, k, xh, z, xl: (y, k, xh, (z + by) % 4, xl))


def along_y(value, by):
    return hop(value, lambda y, k, xh, z, xl: ((y + by) % 4, k, xh, z, xl))


def of_four(value):
    pair = jnp.concatenate([value, beside(value)], 1)
    return jnp.concatenate([pair, other_core(pair)], 1)


def to_four(partial):
    width = partial.shape[1] // 4
    pair = partial[:, : 2 * width] + other_core(partial[:, 2 * width :].astype(BF16)).astype(F32)
    return pair[:, :width] + beside(pair[:, width:].astype(BF16)).astype(F32)


def across(value, same, senders):
    def dest(y, k, xh, z, xl):
        if senders is not None and (k == xl) != senders:
            return None
        return (y, k, xh if same else 1 - xh, z, 1 - xl)

    return hop(value, dest)


def rows(value):
    cut = value.shape[0] // 2 // 8 * 8 + 8
    return value[:cut], value[cut:]


def join(*pieces):
    return jnp.concatenate(pieces, 0)


def total(*terms):
    return sum(t.astype(F32) for t in terms).astype(BF16)


def gather_x(shard, keeper):
    near, far = across(shard, True, True), across(shard, False, True)
    far0, far1 = rows(far)
    back0, back1 = across(far0, True, False), across(rows(near)[1], False, False)
    mine = jnp.where(keeper, shard, near)
    other = jnp.where(keeper, join(back0, back1), far)
    return join(mine, other)


def gather_z(both):
    size = both.shape[0] // 2
    below, above = along_z(both, 1), along_z(both, -1)
    across0, across1 = along_z(below[:size], 1), along_z(above[size:], -1)
    return join(both, above, across0, across1, below)


def sum_z(blocks):
    size = blocks[0][0].shape[0]
    up = along_z(join(blocks[2][0], blocks[1][1]), 1)
    down = along_z(join(blocks[2][1], blocks[3][0]), -1)
    up_last = along_z(total(blocks[1][0], up[:size]), 1)
    down_last = along_z(total(blocks[3][1], down[:size]), -1)
    return total(blocks[0][0], down[size:], up_last), total(blocks[0][1], up[size:], down_last)


def opposite_x(value):
    return hop(value, lambda y, k, xh, z, xl: (y, k, 1 - xh, z, xl))


def both_ways_y(value):
    return along_y(value, 1), along_y(value, -1)


def sum_y(mine, below, above):
    opposite = join(along_y(rows(below)[0], 1), along_y(rows(above)[1], -1))
    added = (mine.astype(F32) + opposite.astype(F32)) + (below.astype(F32) + above.astype(F32))
    return added.astype(BF16)


def exchange(value):
    return lax.all_to_all(value, PLANE, split_axis=0, concat_axis=0, tiled=True)


def dot(left, right, lc, rc):
    return lax.dot_general(left, right, (((lc,), (rc,)), ((), ())), preferred_element_type=F32)


def parts_of(value, count):
    parts = []
    for _ in range(count):
        high = lax.reduce_precision(value, exponent_bits=8, mantissa_bits=7)
        parts.append(high.astype(BF16))
        value = value - high
    return parts


def norm_forward(stream, gain, bias):
    average = jnp.mean(stream, 0, keepdims=True)
    centred = stream - average
    inv_std = lax.rsqrt(jnp.mean(centred * centred, 0, keepdims=True) + epsilon)
    normed = centred * inv_std
    return (normed * gain[:, None] + bias[:, None]).astype(BF16), normed, inv_std


def norm_backward(grad_out, normed, inv_std, gain):
    scaled = grad_out * gain[:, None]
    first = jnp.mean(scaled, 0, keepdims=True)
    second = jnp.mean(scaled * normed, 0, keepdims=True)
    grad_in = inv_std * (scaled - first - normed * second)
    return grad_in, jnp.sum(grad_out * normed, 1), jnp.sum(grad_out, 1)


def gelu_both(value):
    c = math.sqrt(2.0 / math.pi)
    square = value * value
    t = jnp.tanh(c * (value + 0.044715 * value * square))
    out = 0.5 * value * (1.0 + t)
    slope = 0.5 * (1.0 + t) + 0.5 * value * (1.0 - t * t) * c * (1.0 + 3 * 0.044715 * square)
    return out, slope


QB = 256
KB = 512


def turned(block):
    return block.astype(F32).T.astype(BF16)


def key_chunks(last):
    chunks = [(s, min(KB, last - s), False) for s in range(0, last, KB)]
    return chunks + [(last, QB, True)]


def masked(scores, start, low, high):
    keys = lax.broadcasted_iota(jnp.int32, scores.shape, 0) + start
    allowed = keys >= low
    if high is not None:
        allowed = allowed & (keys <= high)
    return jnp.where(allowed, scores, NEG)


def attend_kernel(low_ref, low16_ref, pos16_ref, mixed_ref, q16_ref, out_ref, lse_ref, out16_ref, lse16_ref, qt, kn, vt, kn16, vt16):
    slots, _, width = mixed_ref.shape
    tokens = slots * width
    for s in range(slots):
        at = pl.ds(s * width, width)
        qt[:, at] = (mixed_ref[s, 0:64, :].astype(F32) * 0.125).astype(BF16)
        kn[at, :] = turned(mixed_ref[s, 64:128, :])
        vt[:, at] = mixed_ref[s, 128:192, :]
        kn16[at, :] = turned(mixed_ref[s, 192:256, :])
        vt16[:, at] = mixed_ref[s, 256:320, :]

    def block(q, chunks, keys, values, low, high):
        width = q.shape[1]
        top = jnp.full((1, width), NEG, F32)
        total = jnp.zeros((1, width), F32)
        out = jnp.zeros((HEAD_DIM, width), F32)
        for start, size, diagonal in chunks:
            scores = dot(keys[pl.ds(start, size), :], q, 1, 0) * LOG2E
            scores = masked(scores, start, low, high if diagonal else None)
            higher = jnp.maximum(top, jnp.max(scores, 0, keepdims=True))
            fade = jnp.exp2(top - higher)
            weights = jnp.exp2(scores - higher)
            total = total * fade + jnp.sum(weights, 0, keepdims=True)
            out = out * fade + dot(values[:, pl.ds(start, size)], weights.astype(BF16), 1, 0)
            top = higher
        return out / total, top + jnp.log2(total)

    for b in range(tokens // QB):
        at = pl.ds(b * QB, QB)
        high = lax.broadcasted_iota(jnp.int32, (1, QB), 1) + b * QB
        out, lse = block(qt[:, at], key_chunks(b * QB), kn, vt, low_ref[:, at], high)
        out_ref[:, at] = out
        lse_ref[:, at] = lse
    q16 = (q16_ref[...].astype(F32) * 0.125).astype(BF16)
    chunks = [(s, KB, True) for s in range(0, tokens, KB)]
    out, lse = block(q16, chunks, kn16, vt16, low16_ref[...], pos16_ref[...])
    out16_ref[...] = out
    lse16_ref[...] = lse


def attend_back_kernel(
    low_ref, low16_ref, pos16_ref, mixed_ref, q16_ref, out_ref, lse_ref, out16_ref, lse16_ref, grad_ref, grad16_ref,
    back_ref, dq16_ref, qt, qn, kt, kn, vn, kt16, kn16, vn16, dot_s, don, dk, dv, dk16, dv16,
):
    slots, _, width = mixed_ref.shape
    tokens = slots * width
    for s in range(slots):
        at = pl.ds(s * width, width)
        scaled = (mixed_ref[s, 0:64, :].astype(F32) * 0.125)
        qt[:, at] = scaled.astype(BF16)
        qn[at, :] = scaled.T.astype(BF16)
        kt[:, at] = mixed_ref[s, 64:128, :]
        kn[at, :] = turned(mixed_ref[s, 64:128, :])
        vn[at, :] = turned(mixed_ref[s, 128:192, :])
        kt16[:, at] = mixed_ref[s, 192:256, :]
        kn16[at, :] = turned(mixed_ref[s, 192:256, :])
        vn16[at, :] = turned(mixed_ref[s, 256:320, :])
        dot_s[:, at] = grad_ref[s]
        don[at, :] = turned(grad_ref[s])
    dk[...] = jnp.zeros_like(dk)
    dv[...] = jnp.zeros_like(dv)

    def block(q_t, q_n, do_t, do_n, lse, delta, chunks, k_n, k_t, v_n, dk_ref, dv_ref, low, high, first):
        dq = jnp.zeros((HEAD_DIM, q_t.shape[1]), F32)
        for start, size, diagonal in chunks:
            at = pl.ds(start, size)
            scores = dot(k_n[at, :], q_t, 1, 0) * LOG2E
            scores = masked(scores, start, low, high if diagonal else None)
            probs = jnp.exp2(scores - lse)
            grad_probs = dot(v_n[at, :], do_t, 1, 0)
            grad_scores = (probs * (grad_probs - delta)).astype(BF16)
            grad_k = dot(grad_scores, q_n, 1, 0)
            grad_v = dot(probs.astype(BF16), do_n, 1, 0)
            if first:
                dk_ref[at, :] = grad_k
                dv_ref[at, :] = grad_v
            else:
                dk_ref[at, :] += grad_k
                dv_ref[at, :] += grad_v
            dq = dq + dot(k_t[:, at], grad_scores, 1, 0)
        return dq * 0.125

    for b in range(tokens // QB):
        at = pl.ds(b * QB, QB)
        high = lax.broadcasted_iota(jnp.int32, (1, QB), 1) + b * QB
        delta = jnp.sum(dot_s[:, at].astype(F32) * out_ref[:, at], 0, keepdims=True)
        dq = block(
            qt[:, at], qn[at, :], dot_s[:, at], don[at, :], lse_ref[:, at], delta, key_chunks(b * QB),
            kn, kt, vn, dk, dv, low_ref[:, at], high, False,
        )
        for half in range(QB // width):
            back_ref[b * (QB // width) + half, 0:64, :] = dq[:, half * width : (half + 1) * width].astype(BF16)
    q16 = q16_ref[...].astype(F32) * 0.125
    g16 = grad16_ref[...]
    delta = jnp.sum(g16.astype(F32) * out16_ref[...], 0, keepdims=True)
    chunks = [(s, KB, True) for s in range(0, tokens, KB)]
    dq16_ref[...] = block(
        q16.astype(BF16), q16.T.astype(BF16), g16, turned(g16), lse16_ref[...], delta, chunks,
        kn16, kt16, vn16, dk16, dv16, low16_ref[...], pos16_ref[...], True,
    ).astype(BF16)
    for s in range(slots):
        at = pl.ds(s * width, width)
        back_ref[s, 64:128, :] = dk[at, :].T.astype(BF16)
        back_ref[s, 128:192, :] = dv[at, :].T.astype(BF16)
        back_ref[s, 192:256, :] = dk16[at, :].T.astype(BF16)
        back_ref[s, 256:320, :] = dv16[at, :].T.astype(BF16)


def attend(low, low16, pos16, mixed, q16):
    slots, _, width = mixed.shape
    tokens = slots * width
    shapes = [
        jax.ShapeDtypeStruct((HEAD_DIM, tokens), F32),
        jax.ShapeDtypeStruct((1, tokens), F32),
        jax.ShapeDtypeStruct((HEAD_DIM, width), F32),
        jax.ShapeDtypeStruct((1, width), F32),
    ]
    flat, tall = (HEAD_DIM, tokens), (tokens, HEAD_DIM)
    return pl.pallas_call(
        attend_kernel,
        out_shape=shapes,
        scratch_shapes=[pltpu.VMEM(s, BF16) for s in (flat, tall, flat, tall, flat)],
        compiler_params=pltpu.CompilerParams(vmem_limit_bytes=48 * 2**20),
        cost_estimate=pl.CostEstimate(flops=4 * 10**9, bytes_accessed=4 * 10**6, transcendentals=3 * 10**6),
        name="attend",
    )(low, low16, pos16, mixed, q16)


def attend_back(low, low16, pos16, mixed, q16, out, lse, out16, lse16, grad, grad16):
    slots, _, width = mixed.shape
    tokens = slots * width
    flat, tall = (HEAD_DIM, tokens), (tokens, HEAD_DIM)
    return pl.pallas_call(
        attend_back_kernel,
        out_shape=[
            jax.ShapeDtypeStruct(mixed.shape, BF16),
            jax.ShapeDtypeStruct((HEAD_DIM, width), BF16),
        ],
        scratch_shapes=[pltpu.VMEM(s, BF16) for s in (flat, tall, flat, tall, tall, flat, tall, tall, flat, tall)]
        + [pltpu.VMEM(tall, F32)] * 4,
        compiler_params=pltpu.CompilerParams(vmem_limit_bytes=48 * 2**20),
        cost_estimate=pl.CostEstimate(flops=10 * 10**9, bytes_accessed=5 * 10**6, transcendentals=3 * 10**6),
        name="attend_back",
    )(low, low16, pos16, mixed, q16, out, lse, out16, lse16, grad, grad16)


def to_relative(blocks, xh, z):
    grid = blocks.reshape(2, 4, 2, *blocks.shape[1:])
    grid = jnp.where(xh == 0, grid, grid[::-1])
    grid = lax.dynamic_slice_in_dim(jnp.concatenate([grid, grid], 1), z, 4, 1)
    return grid.swapaxes(0, 1).reshape(blocks.shape)


def from_relative(blocks, xh, z):
    grid = blocks.reshape(4, 2, 2, *blocks.shape[1:]).swapaxes(0, 1)
    grid = lax.dynamic_slice_in_dim(jnp.concatenate([grid, grid], 1), 4 - z, 4, 1)
    grid = jnp.where(xh == 0, grid, grid[::-1])
    return grid.reshape(blocks.shape)


def gather_rows(shard):
    return lax.all_gather(shard, ROW, axis=0, tiled=True)


def local(x_in, segment_ids, gain1, bias1, w_qkv, w_out, gain2, bias2, w_up, w_down, cotangent):
    feats, tokens = x_in.shape
    width = tokens // SLOTS
    d = feats * SLOTS
    core = lax.axis_index("k")
    group = lax.axis_index(("y", "k"))
    slot = lax.axis_index(PLANE)
    first = core == 0
    offset = jnp.sum((segment_ids == segment_ids[0]).astype(jnp.int32))

    xh, z = lax.axis_index("xh"), lax.axis_index("z")
    keeper = lax.axis_index("xl") == core

    qkv_half = w_qkv.shape[2]
    out_half = w_out.shape[2]
    ff_half = w_up.shape[2]
    quarter = -(-ff_half // 256) * 128

    def quarter_of(shard):
        high = jnp.pad(shard[:, quarter:], ((0, 0), (0, 2 * quarter - ff_half)))
        return jnp.where(first, shard[:, :quarter], high)

    w_all = gather_rows(jnp.concatenate([quarter_of(w_up[0]), quarter_of(w_down[0]), match_half(w_out[0])], 1))
    wu, wd, wo = w_all[:, :quarter], w_all[:, quarter : 2 * quarter], w_all[:, 2 * quarter :]
    wq = gather_x(w_qkv[0], keeper)

    def relative(value):
        return to_relative(value.reshape(SLOTS, feats, -1), xh, z).reshape(value.shape)

    def absolute(value):
        return from_relative(value.reshape(SLOTS, feats, -1), xh, z).reshape(value.shape)

    pair = jnp.concatenate([x_in, cotangent.astype(BF16)], 0)
    ahead = to_group(pair[:, : tokens // 4 * 3], -1)
    rotated = lax.dynamic_slice_in_dim(jnp.concatenate([pair, ahead], 1), offset, tokens, 1)
    blocks = rotated.reshape(2 * feats, SLOTS, width).transpose(1, 0, 2)
    vectors = jnp.concatenate([gain1, bias1, gain2, bias2], 0)
    vectors = jnp.concatenate(parts_of(vectors, 3), 0)
    vectors = jnp.pad(vectors, ((0, 0), (0, width - feats)))
    sent = jnp.concatenate([blocks, jnp.broadcast_to(vectors, (SLOTS, *vectors.shape))], 1)
    sent, wq = lax.optimization_barrier((sent, wq))
    wq = gather_z(wq)
    wq_other, wo_other = other_core(wq), other_core(wo)
    got = exchange(sent)
    stream = got[:, :feats].reshape(d, width).astype(F32)
    grad_low = got[:, feats : 2 * feats].reshape(d, width)
    vectors = got[:, 2 * feats :, :feats].astype(F32).reshape(SLOTS, 3, 4, feats).sum(1)
    g1, b1, g2, b2 = vectors.transpose(1, 0, 2).reshape(4, d)
    grad_low_four = of_four(grad_low)

    n1, xhat1, inv1 = norm_forward(stream, g1, b1)
    n1 = relative(n1)
    n1_both = jnp.concatenate([n1, other_core(n1)], 1)
    n1_beside = beside(n1_both)
    n1_four = jnp.concatenate([n1, n1_beside[:, :width], n1_both[:, width:], n1_beside[:, width:]], 1)
    mixed_half = dot(wq, n1_both, 0, 0).astype(BF16)
    mine, theirs = mixed_half[:, :width], other_core(mixed_half[:, width:])
    mixed = jnp.where(first, jnp.concatenate([mine, theirs], 0), jnp.concatenate([theirs, mine], 0))
    many = PAIR_HEADS * HEAD_DIM
    by_head = [mixed[i * d : i * d + many].reshape(SLOTS, HEAD_DIM, width) for i in range(3)]
    last = [mixed[i * d + many : (i + 1) * d] for i in range(3)]
    shared = jnp.broadcast_to(jnp.concatenate(last[1:], 0), (SLOTS, 2 * HEAD_DIM, width))
    heads = exchange(jnp.concatenate(by_head + [shared], 1))
    q16 = last[0]
    positions = jnp.arange(tokens, dtype=jnp.int32)[None]
    border = jnp.where(group == 7, tokens - offset, 0)
    low = jnp.where(positions >= border, border, 0)
    pos16 = jnp.arange(width, dtype=jnp.int32)[None] + slot * width
    low16 = jnp.where(pos16 >= border, border, 0)
    out, lse, out16, lse16 = attend(low, low16, pos16, heads, q16)
    sent = out.astype(BF16).reshape(HEAD_DIM, SLOTS, width).transpose(1, 0, 2)
    attended = jnp.concatenate([exchange(sent).reshape(many, width), out16.astype(BF16)], 0)

    def own_half(value, size):
        return jnp.where(first, value[:size], value[size:]), jnp.where(first, value[size:], value[:size])

    att_mine, att_theirs = own_half(attended, out_half)
    mid = stream + dot(wo, att_mine, 1, 0) + dot(wo_other, att_theirs, 1, 0)

    n2, xhat2, inv2 = norm_forward(mid, g2, b2)
    n2_four = of_four(n2)
    before = dot(wu, n2_four, 0, 0)
    hidden, slope = gelu_both(before)
    hidden = hidden.astype(BF16)
    block_out = mid + to_four(dot(wd, hidden, 1, 0))
    grad_hidden = dot(wd, grad_low_four, 0, 0)
    grad_before = (grad_hidden * slope).astype(BF16)
    grad_n2 = to_four(dot(wu, grad_before, 1, 0))
    grad_up = dot(n2_four, grad_before, 1, 1).astype(BF16)
    grad_down = dot(grad_low_four, hidden, 1, 1).astype(BF16)
    early = jnp.concatenate([grad_up, grad_down], 1)
    grad_n2, early = lax.optimization_barrier((grad_n2, early))
    early = lax.psum_scatter(early, ROW, scatter_dimension=0, tiled=True)
    more, grad_g2, grad_b2 = norm_backward(grad_n2, xhat2, inv2, g2)
    grad = grad_low.astype(F32) + more

    grad_mid = grad.astype(BF16)
    part, part_other = dot(wo, grad_mid, 0, 0).astype(BF16), dot(wo_other, grad_mid, 0, 0).astype(BF16)
    grad_att = jnp.where(first, jnp.concatenate([part, part_other], 0), jnp.concatenate([part_other, part], 0))
    grad_heads = exchange(grad_att[:many].reshape(SLOTS, HEAD_DIM, width))
    grad_heads, dq16 = attend_back(low, low16, pos16, heads, q16, out, lse, out16, lse16, grad_heads, grad_att[many:])
    got = exchange(grad_heads)
    pieces = [got[:, i * HEAD_DIM : (i + 1) * HEAD_DIM].reshape(many, width) for i in range(3)]
    shared = got[:, 3 * HEAD_DIM :].astype(F32).sum(0).astype(BF16)
    grad_mixed = jnp.concatenate(
        [pieces[0], dq16, pieces[1], shared[:HEAD_DIM], pieces[2], shared[HEAD_DIM:]], 0
    )
    gm_mine, gm_theirs = own_half(grad_mixed, qkv_half)
    cut = qkv_half // 256 * 128 + 128
    out_cut = quarter - cut
    left = lax.axis_index("xl") == 0

    def four_rows(value, size):
        low, high = value[: value.shape[0] // 2], value[value.shape[0] // 2 :]
        pair = jnp.concatenate([jnp.where(left, low, high), beside(jnp.where(left, high, low))], 1)
        room = max(size, pair.shape[0] - size)
        low, high = (jnp.pad(v, ((0, room - v.shape[0]), (0, 0))) for v in (pair[:size], pair[size:]))
        return jnp.concatenate([jnp.where(first, low, high), other_core(jnp.where(first, high, low))], 1)

    gm_four, att_four = four_rows(grad_mixed, cut), four_rows(attended, out_cut)
    rest, out_rest = qkv_half - cut, out_half - out_cut
    zeros = functools.partial(jnp.zeros, dtype=BF16)
    count = 4 * width
    right_qkv = jnp.where(
        first,
        join(gm_four, zeros((quarter - cut, count))),
        join(gm_four[:rest], zeros((quarter - rest, count))),
    )
    right_out = jnp.where(
        first,
        join(zeros((cut, count)), att_four[:out_cut]),
        join(zeros((rest, count)), att_four[:out_rest], zeros((quarter - rest - out_rest, count))),
    )
    grad_mid_four = relative(of_four(grad_mid))
    late = (dot(grad_mid_four, right_out, 1, 1) + dot(n1_four, right_qkv, 1, 1)).astype(BF16)
    size = d // 8
    mine, other = sum_z([[late[(2 * i + e) * size : (2 * i + e + 1) * size] for e in range(2)] for i in range(4)])
    other, early = lax.optimization_barrier((other, early))
    early_two = both_ways_y(early)
    late = total(mine, opposite_x(other))
    late, early_two = lax.optimization_barrier((late, early_two))
    early = sum_y(early, *early_two)
    late = sum_y(late, *both_ways_y(late))
    grad_n1 = absolute(dot(wq, gm_mine, 1, 0) + dot(wq_other, gm_theirs, 1, 0))
    more, grad_g1, grad_b1 = norm_backward(grad_n1, xhat1, inv1, g1)
    grad = grad + more

    mine = jnp.concatenate([early, late], 1)
    theirs = other_core(mine)
    low, high = jnp.where(first, mine, theirs), jnp.where(first, theirs, mine)

    def columns(at, size, high_at, high_size):
        return jnp.concatenate([low[:, at : at + size], high[:, high_at : high_at + high_size]], 1).astype(F32)[None]

    high_size = ff_half - quarter
    grad_up = columns(0, quarter, 0, high_size)
    grad_down = columns(quarter, quarter, quarter, high_size)
    grad_wq = columns(2 * quarter, cut, 2 * quarter, rest)
    grad_wo = columns(2 * quarter + cut, out_cut, 2 * quarter + rest, out_rest)

    vectors = jnp.stack([grad_g1, grad_b1, grad_g2, grad_b2]).reshape(4, SLOTS, feats).transpose(1, 0, 2)
    vectors = jnp.pad(jnp.concatenate(parts_of(vectors, 2), 1), ((0, 0), (0, 0), (0, width - feats)))
    sent = jnp.concatenate(
        [block_out.astype(BF16).reshape(SLOTS, feats, width), grad.astype(BF16).reshape(SLOTS, feats, width), vectors], 1
    )
    got = exchange(sent)
    vectors = got[:, 2 * feats :, :feats].astype(F32).reshape(SLOTS, 2, 4, feats).sum((0, 1))
    vectors = vectors + other_core(vectors)
    turns = [hop(vectors, lambda y, k, xh, z, xl, by=by: ((y + by) % 4, k, xh, z, xl)) for by in (1, 2, 3)]
    vectors = (vectors + turns[1]) + (turns[0] + turns[2])
    pair = got[:, : 2 * feats].transpose(1, 0, 2).reshape(2 * feats, tokens)
    behind = to_group(pair[:, tokens // 4 :], 1)
    both = jnp.concatenate([behind, pair], 1)
    pair = lax.dynamic_slice_in_dim(both, tokens // 4 * 3 - offset, tokens, 1).astype(F32)
    return (
        pair[:feats],
        pair[feats:],
        vectors[0][None],
        vectors[1][None],
        grad_wq,
        grad_wo,
        vectors[2][None],
        vectors[3][None],
        grad_up,
        grad_down,
    )


def solution(mesh):
    grid = Mesh(mesh.devices.reshape(SIZES), AXES)
    stream = P(PLANE, ("y", "k"))
    vector = P(None, PLANE)
    weight = P(None, ROW, "xl")
    return jax.shard_map(
        local,
        mesh=grid,
        in_specs=(stream, P(), vector, vector, weight, weight, vector, vector, weight, weight, stream),
        out_specs=(stream, stream, vector, vector, weight, weight, vector, vector, weight, weight),
        check_vma=False,
    )
```

```python
import functools
import itertools
import math

import jax
import jax.numpy as jnp
from jax import lax
from jax.experimental import pallas as pl
from jax.experimental.pallas import tpu as pltpu
from jax.sharding import Mesh, PartitionSpec as P

HEADS = 17
HEAD_DIM = 64
PAIR_HEADS = HEADS - 1
epsilon = 1e-05
LOG2E = math.log2(math.e)
NEG = -1e30
AXES = ("y", "k", "xh", "z", "xl")
SIZES = (4, 2, 2, 4, 2)
PLANE = ("xh", "z", "xl")
ROW = ("xh", "z")
SLOTS = 16
F32 = jnp.float32
BF16 = jnp.bfloat16


def hop(value, dest):
    spots = list(itertools.product(*[range(s) for s in SIZES]))
    at = {c: i for i, c in enumerate(spots)}
    pairs = [(at[c], at[dest(*c)]) for c in spots if dest(*c) is not None]
    return lax.ppermute(value, AXES, pairs)


def other_core(value):
    return hop(value, lambda y, k, xh, z, xl: (y, 1 - k, xh, z, xl))


def to_group(value, by):
    def dest(y, k, xh, z, xl):
        g = (2 * y + k + by) % 8
        return (g // 2, g % 2, xh, z, xl)

    return hop(value, dest)


def match_half(value):
    def dest(y, k, xh, z, xl):
        return (y, k, xh, z, xl) if k == xl else (y, 1 - k, xh, z, 1 - xl)

    return hop(value, dest)


def beside(value):
    return hop(value, lambda y, k, xh, z, xl: (y, k, xh, z, 1 - xl))


def along_z(value, by):
    return hop(value, lambda y, k, xh, z, xl: (y, k, xh, (z + by) % 4, xl))


def along_y(value, by):
    return hop(value, lambda y, k, xh, z, xl: ((y + by) % 4, k, xh, z, xl))


def of_four(value):
    pair = jnp.concatenate([value, beside(value)], 1)
    return jnp.concatenate([pair, other_core(pair)], 1)


def to_four(partial):
    width = partial.shape[1] // 4
    pair = partial[:, : 2 * width] + other_core(partial[:, 2 * width :].astype(BF16)).astype(F32)
    return pair[:, :width] + beside(pair[:, width:].astype(BF16)).astype(F32)


def rows(value):
    cut = value.shape[0] // 2 // 8 * 8 + 8
    return value[:cut], value[cut:]


def join(*pieces):
    return jnp.concatenate(pieces, 0)


def total(*terms):
    return sum(t.astype(F32) for t in terms).astype(BF16)


def gather_z(both):
    size = both.shape[0] // 2
    below, above = along_z(both, 1), along_z(both, -1)
    across0, across1 = along_z(below[:size], 1), along_z(above[size:], -1)
    return join(both, above, across0, across1, below)


def sum_z(blocks):
    size = blocks[0][0].shape[0]
    up = along_z(join(blocks[2][0], blocks[1][1]), 1)
    down = along_z(join(blocks[2][1], blocks[3][0]), -1)
    up_last = along_z(total(blocks[1][0], up[:size]), 1)
    down_last = along_z(total(blocks[3][1], down[:size]), -1)
    return total(blocks[0][0], down[size:], up_last), total(blocks[0][1], up[size:], down_last)


def opposite_x(value):
    return hop(value, lambda y, k, xh, z, xl: (y, k, 1 - xh, z, xl))


def both_ways_y(value):
    return along_y(value, 1), along_y(value, -1)


def sum_y(mine, below, above):
    opposite = join(along_y(rows(below)[0], 1), along_y(rows(above)[1], -1))
    added = (mine.astype(F32) + opposite.astype(F32)) + (below.astype(F32) + above.astype(F32))
    return added.astype(BF16)


def exchange(value):
    return lax.all_to_all(value, PLANE, split_axis=0, concat_axis=0, tiled=True)


def dot(left, right, lc, rc):
    return lax.dot_general(left, right, (((lc,), (rc,)), ((), ())), preferred_element_type=F32)


def parts_of(value, count):
    parts = []
    for _ in range(count):
        high = lax.reduce_precision(value, exponent_bits=8, mantissa_bits=7)
        parts.append(high.astype(BF16))
        value = value - high
    return parts


def norm_forward(stream, gain, bias):
    average = jnp.mean(stream, 0, keepdims=True)
    centred = stream - average
    inv_std = lax.rsqrt(jnp.mean(centred * centred, 0, keepdims=True) + epsilon)
    normed = centred * inv_std
    return (normed * gain[:, None] + bias[:, None]).astype(BF16), normed, inv_std


def norm_backward(grad_out, normed, inv_std, gain):
    scaled = grad_out * gain[:, None]
    first = jnp.mean(scaled, 0, keepdims=True)
    second = jnp.mean(scaled * normed, 0, keepdims=True)
    grad_in = inv_std * (scaled - first - normed * second)
    return grad_in, jnp.sum(grad_out * normed, 1), jnp.sum(grad_out, 1)


def gelu_both(value):
    c = math.sqrt(2.0 / math.pi)
    square = value * value
    t = jnp.tanh(c * (value + 0.044715 * value * square))
    out = 0.5 * value * (1.0 + t)
    slope = 0.5 * (1.0 + t) + 0.5 * value * (1.0 - t * t) * c * (1.0 + 3 * 0.044715 * square)
    return out, slope


QB = 256
KB = 512


def turned(block):
    return block.astype(F32).T.astype(BF16)


def key_chunks(last):
    chunks = [(s, min(KB, last - s), False) for s in range(0, last, KB)]
    return chunks + [(last, QB, True)]


def masked(scores, start, low, high):
    keys = lax.broadcasted_iota(jnp.int32, scores.shape, 0) + start
    allowed = keys >= low
    if high is not None:
        allowed = allowed & (keys <= high)
    return jnp.where(allowed, scores, NEG)


def attend_kernel(low_ref, low16_ref, pos16_ref, mixed_ref, q16_ref, out_ref, lse_ref, out16_ref, lse16_ref, qt, kn, vt, kn16, vt16):
    slots, _, width = mixed_ref.shape
    tokens = slots * width
    for s in range(slots):
        at = pl.ds(s * width, width)
        qt[:, at] = (mixed_ref[s, 0:64, :].astype(F32) * 0.125).astype(BF16)
        kn[at, :] = turned(mixed_ref[s, 64:128, :])
        vt[:, at] = mixed_ref[s, 128:192, :]
        kn16[at, :] = turned(mixed_ref[s, 192:256, :])
        vt16[:, at] = mixed_ref[s, 256:320, :]

    def block(q, chunks, keys, values, low, high):
        width = q.shape[1]
        top = jnp.full((1, width), NEG, F32)
        total = jnp.zeros((1, width), F32)
        out = jnp.zeros((HEAD_DIM, width), F32)
        for start, size, diagonal in chunks:
            scores = dot(keys[pl.ds(start, size), :], q, 1, 0) * LOG2E
            scores = masked(scores, start, low, high if diagonal else None)
            higher = jnp.maximum(top, jnp.max(scores, 0, keepdims=True))
            fade = jnp.exp2(top - higher)
            weights = jnp.exp2(scores - higher)
            total = total * fade + jnp.sum(weights, 0, keepdims=True)
            out = out * fade + dot(values[:, pl.ds(start, size)], weights.astype(BF16), 1, 0)
            top = higher
        return out / total, top + jnp.log2(total)

    for b in range(tokens // QB):
        at = pl.ds(b * QB, QB)
        high = lax.broadcasted_iota(jnp.int32, (1, QB), 1) + b * QB
        out, lse = block(qt[:, at], key_chunks(b * QB), kn, vt, low_ref[:, at], high)
        out_ref[:, at] = out
        lse_ref[:, at] = lse
    q16 = (q16_ref[...].astype(F32) * 0.125).astype(BF16)
    chunks = [(s, KB, True) for s in range(0, tokens, KB)]
    out, lse = block(q16, chunks, kn16, vt16, low16_ref[...], pos16_ref[...])
    out16_ref[...] = out
    lse16_ref[...] = lse


def attend_back_kernel(
    low_ref, low16_ref, pos16_ref, mixed_ref, q16_ref, out_ref, lse_ref, out16_ref, lse16_ref, grad_ref, grad16_ref,
    back_ref, dq16_ref, qt, qn, kt, kn, vn, kt16, kn16, vn16, dot_s, don, dk, dv, dk16, dv16,
):
    slots, _, width = mixed_ref.shape
    tokens = slots * width
    for s in range(slots):
        at = pl.ds(s * width, width)
        scaled = (mixed_ref[s, 0:64, :].astype(F32) * 0.125)
        qt[:, at] = scaled.astype(BF16)
        qn[at, :] = scaled.T.astype(BF16)
        kt[:, at] = mixed_ref[s, 64:128, :]
        kn[at, :] = turned(mixed_ref[s, 64:128, :])
        vn[at, :] = turned(mixed_ref[s, 128:192, :])
        kt16[:, at] = mixed_ref[s, 192:256, :]
        kn16[at, :] = turned(mixed_ref[s, 192:256, :])
        vn16[at, :] = turned(mixed_ref[s, 256:320, :])
        dot_s[:, at] = grad_ref[s]
        don[at, :] = turned(grad_ref[s])
    dk[...] = jnp.zeros_like(dk)
    dv[...] = jnp.zeros_like(dv)

    def block(q_t, q_n, do_t, do_n, lse, delta, chunks, k_n, k_t, v_n, dk_ref, dv_ref, low, high, first):
        dq = jnp.zeros((HEAD_DIM, q_t.shape[1]), F32)
        for start, size, diagonal in chunks:
            at = pl.ds(start, size)
            scores = dot(k_n[at, :], q_t, 1, 0) * LOG2E
            scores = masked(scores, start, low, high if diagonal else None)
            probs = jnp.exp2(scores - lse)
            grad_probs = dot(v_n[at, :], do_t, 1, 0)
            grad_scores = (probs * (grad_probs - delta)).astype(BF16)
            grad_k = dot(grad_scores, q_n, 1, 0)
            grad_v = dot(probs.astype(BF16), do_n, 1, 0)
            if first:
                dk_ref[at, :] = grad_k
                dv_ref[at, :] = grad_v
            else:
                dk_ref[at, :] += grad_k
                dv_ref[at, :] += grad_v
            dq = dq + dot(k_t[:, at], grad_scores, 1, 0)
        return dq * 0.125

    for b in range(tokens // QB):
        at = pl.ds(b * QB, QB)
        high = lax.broadcasted_iota(jnp.int32, (1, QB), 1) + b * QB
        delta = jnp.sum(dot_s[:, at].astype(F32) * out_ref[:, at], 0, keepdims=True)
        dq = block(
            qt[:, at], qn[at, :], dot_s[:, at], don[at, :], lse_ref[:, at], delta, key_chunks(b * QB),
            kn, kt, vn, dk, dv, low_ref[:, at], high, False,
        )
        for half in range(QB // width):
            back_ref[b * (QB // width) + half, 0:64, :] = dq[:, half * width : (half + 1) * width].astype(BF16)
    q16 = q16_ref[...].astype(F32) * 0.125
    g16 = grad16_ref[...]
    delta = jnp.sum(g16.astype(F32) * out16_ref[...], 0, keepdims=True)
    chunks = [(s, KB, True) for s in range(0, tokens, KB)]
    dq16_ref[...] = block(
        q16.astype(BF16), q16.T.astype(BF16), g16, turned(g16), lse16_ref[...], delta, chunks,
        kn16, kt16, vn16, dk16, dv16, low16_ref[...], pos16_ref[...], True,
    ).astype(BF16)
    for s in range(slots):
        at = pl.ds(s * width, width)
        back_ref[s, 64:128, :] = dk[at, :].T.astype(BF16)
        back_ref[s, 128:192, :] = dv[at, :].T.astype(BF16)
        back_ref[s, 192:256, :] = dk16[at, :].T.astype(BF16)
        back_ref[s, 256:320, :] = dv16[at, :].T.astype(BF16)


def attend(low, low16, pos16, mixed, q16):
    slots, _, width = mixed.shape
    tokens = slots * width
    shapes = [
        jax.ShapeDtypeStruct((HEAD_DIM, tokens), F32),
        jax.ShapeDtypeStruct((1, tokens), F32),
        jax.ShapeDtypeStruct((HEAD_DIM, width), F32),
        jax.ShapeDtypeStruct((1, width), F32),
    ]
    flat, tall = (HEAD_DIM, tokens), (tokens, HEAD_DIM)
    return pl.pallas_call(
        attend_kernel,
        out_shape=shapes,
        scratch_shapes=[pltpu.VMEM(s, BF16) for s in (flat, tall, flat, tall, flat)],
        compiler_params=pltpu.CompilerParams(vmem_limit_bytes=48 * 2**20),
        cost_estimate=pl.CostEstimate(flops=4 * 10**9, bytes_accessed=4 * 10**6, transcendentals=3 * 10**6),
        name="attend",
    )(low, low16, pos16, mixed, q16)


def attend_back(low, low16, pos16, mixed, q16, out, lse, out16, lse16, grad, grad16):
    slots, _, width = mixed.shape
    tokens = slots * width
    flat, tall = (HEAD_DIM, tokens), (tokens, HEAD_DIM)
    return pl.pallas_call(
        attend_back_kernel,
        out_shape=[
            jax.ShapeDtypeStruct(mixed.shape, BF16),
            jax.ShapeDtypeStruct((HEAD_DIM, width), BF16),
        ],
        scratch_shapes=[pltpu.VMEM(s, BF16) for s in (flat, tall, flat, tall, tall, flat, tall, tall, flat, tall)]
        + [pltpu.VMEM(tall, F32)] * 4,
        compiler_params=pltpu.CompilerParams(vmem_limit_bytes=48 * 2**20),
        cost_estimate=pl.CostEstimate(flops=10 * 10**9, bytes_accessed=5 * 10**6, transcendentals=3 * 10**6),
        name="attend_back",
    )(low, low16, pos16, mixed, q16, out, lse, out16, lse16, grad, grad16)


def to_relative(blocks, xh, z):
    grid = blocks.reshape(2, 4, 2, *blocks.shape[1:])
    grid = jnp.where(xh == 0, grid, grid[::-1])
    grid = lax.dynamic_slice_in_dim(jnp.concatenate([grid, grid], 1), z, 4, 1)
    return grid.swapaxes(0, 1).reshape(blocks.shape)


def from_relative(blocks, xh, z):
    grid = blocks.reshape(4, 2, 2, *blocks.shape[1:]).swapaxes(0, 1)
    grid = lax.dynamic_slice_in_dim(jnp.concatenate([grid, grid], 1), 4 - z, 4, 1)
    grid = jnp.where(xh == 0, grid, grid[::-1])
    return grid.reshape(blocks.shape)


def gather_rows(shard):
    return lax.all_gather(shard, ROW, axis=0, tiled=True)


def local(x_in, segment_ids, gain1, bias1, w_qkv, w_out, gain2, bias2, w_up, w_down, cotangent):
    feats, tokens = x_in.shape
    width = tokens // SLOTS
    d = feats * SLOTS
    core = lax.axis_index("k")
    group = lax.axis_index(("y", "k"))
    slot = lax.axis_index(PLANE)
    first = core == 0
    offset = jnp.sum((segment_ids == segment_ids[0]).astype(jnp.int32))

    xh, z = lax.axis_index("xh"), lax.axis_index("z")
    keeper = lax.axis_index("xl") == core

    qkv_half = w_qkv.shape[2]
    out_half = w_out.shape[2]
    ff_half = w_up.shape[2]
    quarter = -(-ff_half // 256) * 128

    def quarter_of(shard):
        high = jnp.pad(shard[:, quarter:], ((0, 0), (0, 2 * quarter - ff_half)))
        return jnp.where(first, shard[:, :quarter], high)

    w_all = gather_rows(jnp.concatenate([quarter_of(w_up[0]), quarter_of(w_down[0]), match_half(w_out[0])], 1))
    wu, wd, wo = w_all[:, :quarter], w_all[:, quarter : 2 * quarter], w_all[:, 2 * quarter :]
    cut = qkv_half // 256 * 128 + 128
    rest = qkv_half - cut
    left = lax.axis_index("xl") == 0
    shard = jnp.where(first, w_qkv[0, :, :cut], jnp.pad(w_qkv[0, :, cut:], ((0, 0), (0, cut - rest))))
    wq = join(shard, opposite_x(shard))

    def relative(value):
        return to_relative(value.reshape(SLOTS, feats, -1), xh, z).reshape(value.shape)

    def absolute(value):
        return from_relative(value.reshape(SLOTS, feats, -1), xh, z).reshape(value.shape)

    pair = jnp.concatenate([x_in, cotangent.astype(BF16)], 0)
    ahead = to_group(pair[:, : tokens // 4 * 3], -1)
    rotated = lax.dynamic_slice_in_dim(jnp.concatenate([pair, ahead], 1), offset, tokens, 1)
    blocks = rotated.reshape(2 * feats, SLOTS, width).transpose(1, 0, 2)
    vectors = jnp.concatenate([gain1, bias1, gain2, bias2], 0)
    vectors = jnp.concatenate(parts_of(vectors, 3), 0)
    vectors = jnp.pad(vectors, ((0, 0), (0, width - feats)))
    sent = jnp.concatenate([blocks, jnp.broadcast_to(vectors, (SLOTS, *vectors.shape))], 1)
    sent, wq = lax.optimization_barrier((sent, wq))
    wq = gather_z(wq)
    wo_other = other_core(wo)
    got = exchange(sent)
    stream = got[:, :feats].reshape(d, width).astype(F32)
    grad_low = got[:, feats : 2 * feats].reshape(d, width)
    vectors = got[:, 2 * feats :, :feats].astype(F32).reshape(SLOTS, 3, 4, feats).sum(1)
    g1, b1, g2, b2 = vectors.transpose(1, 0, 2).reshape(4, d)
    grad_low_four = of_four(grad_low)

    n1, xhat1, inv1 = norm_forward(stream, g1, b1)
    n1_four = of_four(relative(n1))
    quarter_four = dot(wq, n1_four, 0, 0).astype(BF16)
    mine, theirs = quarter_four[:, : 2 * width], other_core(quarter_four[:, 2 * width :])
    half = jnp.where(first, join(mine, theirs[:rest]), join(theirs, mine[:rest]))
    mine, theirs = half[:, :width], beside(half[:, width:])
    mixed = jnp.where(left, join(mine, theirs), join(theirs, mine))
    many = PAIR_HEADS * HEAD_DIM
    by_head = [mixed[i * d : i * d + many].reshape(SLOTS, HEAD_DIM, width) for i in range(3)]
    last = [mixed[i * d + many : (i + 1) * d] for i in range(3)]
    shared = jnp.broadcast_to(jnp.concatenate(last[1:], 0), (SLOTS, 2 * HEAD_DIM, width))
    heads = exchange(jnp.concatenate(by_head + [shared], 1))
    q16 = last[0]
    positions = jnp.arange(tokens, dtype=jnp.int32)[None]
    border = jnp.where(group == 7, tokens - offset, 0)
    low = jnp.where(positions >= border, border, 0)
    pos16 = jnp.arange(width, dtype=jnp.int32)[None] + slot * width
    low16 = jnp.where(pos16 >= border, border, 0)
    out, lse, out16, lse16 = attend(low, low16, pos16, heads, q16)
    sent = out.astype(BF16).reshape(HEAD_DIM, SLOTS, width).transpose(1, 0, 2)
    attended = jnp.concatenate([exchange(sent).reshape(many, width), out16.astype(BF16)], 0)

    def own_half(value, size):
        return jnp.where(first, value[:size], value[size:]), jnp.where(first, value[size:], value[:size])

    att_mine, att_theirs = own_half(attended, out_half)
    mid = stream + dot(wo, att_mine, 1, 0) + dot(wo_other, att_theirs, 1, 0)

    n2, xhat2, inv2 = norm_forward(mid, g2, b2)
    n2_four = of_four(n2)
    before = dot(wu, n2_four, 0, 0)
    hidden, slope = gelu_both(before)
    hidden = hidden.astype(BF16)
    block_out = mid + to_four(dot(wd, hidden, 1, 0))
    grad_hidden = dot(wd, grad_low_four, 0, 0)
    grad_before = (grad_hidden * slope).astype(BF16)
    grad_n2 = to_four(dot(wu, grad_before, 1, 0))
    grad_up = dot(n2_four, grad_before, 1, 1).astype(BF16)
    grad_down = dot(grad_low_four, hidden, 1, 1).astype(BF16)
    early = jnp.concatenate([grad_up, grad_down], 1)
    grad_n2, early = lax.optimization_barrier((grad_n2, early))
    early = lax.psum_scatter(early, ROW, scatter_dimension=0, tiled=True)
    more, grad_g2, grad_b2 = norm_backward(grad_n2, xhat2, inv2, g2)
    grad = grad_low.astype(F32) + more

    grad_mid = grad.astype(BF16)
    part, part_other = dot(wo, grad_mid, 0, 0).astype(BF16), dot(wo_other, grad_mid, 0, 0).astype(BF16)
    grad_att = jnp.where(first, jnp.concatenate([part, part_other], 0), jnp.concatenate([part_other, part], 0))
    grad_heads = exchange(grad_att[:many].reshape(SLOTS, HEAD_DIM, width))
    grad_heads, dq16 = attend_back(low, low16, pos16, heads, q16, out, lse, out16, lse16, grad_heads, grad_att[many:])
    got = exchange(grad_heads)
    pieces = [got[:, i * HEAD_DIM : (i + 1) * HEAD_DIM].reshape(many, width) for i in range(3)]
    shared = got[:, 3 * HEAD_DIM :].astype(F32).sum(0).astype(BF16)
    grad_mixed = jnp.concatenate(
        [pieces[0], dq16, pieces[1], shared[:HEAD_DIM], pieces[2], shared[HEAD_DIM:]], 0
    )
    out_cut = quarter - cut

    def four_rows(value, size):
        low, high = value[: value.shape[0] // 2], value[value.shape[0] // 2 :]
        pair = jnp.concatenate([jnp.where(left, low, high), beside(jnp.where(left, high, low))], 1)
        room = max(size, pair.shape[0] - size)
        low, high = (jnp.pad(v, ((0, room - v.shape[0]), (0, 0))) for v in (pair[:size], pair[size:]))
        return jnp.concatenate([jnp.where(first, low, high), other_core(jnp.where(first, high, low))], 1)

    gm_four, att_four = four_rows(grad_mixed, cut), four_rows(attended, out_cut)
    out_rest = out_half - out_cut
    zeros = functools.partial(jnp.zeros, dtype=BF16)
    count = 4 * width
    right_qkv = jnp.where(
        first,
        join(gm_four, zeros((quarter - cut, count))),
        join(gm_four[:rest], zeros((quarter - rest, count))),
    )
    right_out = jnp.where(
        first,
        join(zeros((cut, count)), att_four[:out_cut]),
        join(zeros((rest, count)), att_four[:out_rest], zeros((quarter - rest - out_rest, count))),
    )
    grad_mid_four = relative(of_four(grad_mid))
    late = (dot(grad_mid_four, right_out, 1, 1) + dot(n1_four, right_qkv, 1, 1)).astype(BF16)
    size = d // 8
    mine, other = sum_z([[late[(2 * i + e) * size : (2 * i + e + 1) * size] for e in range(2)] for i in range(4)])
    other, early = lax.optimization_barrier((other, early))
    early_two = both_ways_y(early)
    late = total(mine, opposite_x(other))
    late, early_two = lax.optimization_barrier((late, early_two))
    early = sum_y(early, *early_two)
    late = sum_y(late, *both_ways_y(late))
    grad_n1 = absolute(to_four(dot(wq, gm_four, 1, 0)))
    more, grad_g1, grad_b1 = norm_backward(grad_n1, xhat1, inv1, g1)
    grad = grad + more

    mine = jnp.concatenate([early, late], 1)
    theirs = other_core(mine)
    low, high = jnp.where(first, mine, theirs), jnp.where(first, theirs, mine)

    def columns(at, size, high_at, high_size):
        return jnp.concatenate([low[:, at : at + size], high[:, high_at : high_at + high_size]], 1).astype(F32)[None]

    high_size = ff_half - quarter
    grad_up = columns(0, quarter, 0, high_size)
    grad_down = columns(quarter, quarter, quarter, high_size)
    grad_wq = columns(2 * quarter, cut, 2 * quarter, rest)
    grad_wo = columns(2 * quarter + cut, out_cut, 2 * quarter + rest, out_rest)

    vectors = jnp.stack([grad_g1, grad_b1, grad_g2, grad_b2]).reshape(4, SLOTS, feats).transpose(1, 0, 2)
    vectors = jnp.pad(jnp.concatenate(parts_of(vectors, 2), 1), ((0, 0), (0, 0), (0, width - feats)))
    sent = jnp.concatenate(
        [block_out.astype(BF16).reshape(SLOTS, feats, width), grad.astype(BF16).reshape(SLOTS, feats, width), vectors], 1
    )
    got = exchange(sent)
    vectors = got[:, 2 * feats :, :feats].astype(F32).reshape(SLOTS, 2, 4, feats).sum((0, 1))
    vectors = vectors + other_core(vectors)
    turns = [hop(vectors, lambda y, k, xh, z, xl, by=by: ((y + by) % 4, k, xh, z, xl)) for by in (1, 2, 3)]
    vectors = (vectors + turns[1]) + (turns[0] + turns[2])
    pair = got[:, : 2 * feats].transpose(1, 0, 2).reshape(2 * feats, tokens)
    behind = to_group(pair[:, tokens // 4 :], 1)
    both = jnp.concatenate([behind, pair], 1)
    pair = lax.dynamic_slice_in_dim(both, tokens // 4 * 3 - offset, tokens, 1).astype(F32)
    return (
        pair[:feats],
        pair[feats:],
        vectors[0][None],
        vectors[1][None],
        grad_wq,
        grad_wo,
        vectors[2][None],
        vectors[3][None],
        grad_up,
        grad_down,
    )


def solution(mesh):
    grid = Mesh(mesh.devices.reshape(SIZES), AXES)
    stream = P(PLANE, ("y", "k"))
    vector = P(None, PLANE)
    weight = P(None, ROW, "xl")
    return jax.shard_map(
        local,
        mesh=grid,
        in_specs=(stream, P(), vector, vector, weight, weight, vector, vector, weight, weight, stream),
        out_specs=(stream, stream, vector, vector, weight, weight, vector, vector, weight, weight),
        check_vma=False,
    )
```
